1024 devices in a mesh: grp: 128 (over x, z, core), leaf: 8 (over y).
Axes of the slice: x: 4, y: 8, z: 16, core: 2. Of those that a mesh axis runs over, the one named last changes fastest.
Arguments:
- inputs: float32 [2097152, 64], P(('grp', 'leaf')), may hold values from -6 to 6
- freqs: float32 [64, 256], replicated, may hold values from -0.75 to 0.75
- phases: float32 [256], replicated, may hold values from -3.140625 to 3.140625
- sample_weight: float32 [2097152], P(('grp', 'leaf')), as said below
- stored: float32 [1024, 256, 256], P(('grp', 'leaf')), as said below
- root: int32 [1024], replicated, may hold values from 0 to 1023, each once
Outputs:
- factor: float32 [256, 256], replicated
- basis: float32 [2097152, 256], P(('grp', 'leaf'))
The draws below stay inside these ranges and needn't reach their ends.
Inputs may be any that keep to these rules, and one draw needn't show every extreme that they name: `root`: each device index once, in the order grp first, leaf second; only the first entry is read. `stored`: each slot is upper triangular with a positive diagonal. `sample_weight`: positive row weights.
All inputs are finite; a program needn't handle non-finite values.
Results may differ from the reference program's by a relative error of at most 0.0003.
Values sent between devices are 32-bit elements; how exact they have to be, the bound alone decides.
A program may use at most 32 MiB of HBM per device.

```python
import math
import jax
import jax.numpy as jnp
from jax import lax

IN_DIM = 64
FEATS = 256
ROWS_DEV = 2048
SLOTS = 1024
ROWS = 2097152


def draw_sample_weight(key, part):
    position = jnp.arange(ROWS).astype(jnp.float32) / ROWS
    rise = jnp.exp(math.log(3.0) * position)
    noise = jnp.exp(jax.random.uniform(key, (ROWS,), jnp.float32, -math.log(3.0), math.log(3.0)))
    return (rise * noise).astype(jnp.float32)


def draw_stored(key, part):
    key_diag = jax.random.fold_in(key, 11)
    key_off = jax.random.fold_in(key, 12)
    diag = jnp.exp(jax.random.uniform(key_diag, (SLOTS, FEATS), jnp.float32, math.log(0.2), math.log(2.0)))
    off = jax.random.uniform(key_off, (SLOTS, FEATS, FEATS), jnp.float32, -1.0, 1.0) * 0.5
    row_idx = jnp.arange(FEATS)[:, None]
    col_idx = jnp.arange(FEATS)[None, :]
    upper = (col_idx > row_idx).astype(jnp.float32)
    eye = (col_idx == row_idx).astype(jnp.float32)
    scaled = off * diag[:, :, None] / math.sqrt(FEATS) * upper[None, :, :]
    return (scaled + diag[:, :, None] * eye[None, :, :]).astype(jnp.float32)


def levels(stream_key, shape, split, low, high):
    def one(axis_at, parts):
        steps = jax.random.uniform(jax.random.fold_in(jax.random.fold_in(stream_key, 6), axis_at), (parts,), jnp.float32, low / len(split), high / len(split))
        return jnp.repeat(jnp.exp(steps), shape[axis_at] // parts).reshape((-1,) + (1,) * (len(shape) - axis_at - 1))

    factor_of = one(*split[0])
    for cut in split[1:]:
        factor_of = factor_of * one(*cut)
    return factor_of


def scatter_about(key, extent, width, reach, shards=(), dtype=jnp.bfloat16):
    entries = width * jax.random.normal(key, extent, jnp.float32)
    if shards:
        entries = entries * levels(key, extent, shards, -0.22, 0.18)
    return jnp.clip(entries, -reach, reach).astype(dtype)


def setup_inputs(seed: int = 0) -> dict:
    seeds = jax.random.split(jax.random.key(seed), 7)
    return {
        "inputs": scatter_about(seeds[0], (ROWS, IN_DIM), 1.0, 6.0, ((0, 1024),), jnp.float32),
        "freqs": scatter_about(seeds[1], (IN_DIM, FEATS), IN_DIM ** -0.5, 0.75, (), jnp.float32),
        "phases": jnp.clip(jax.random.uniform(seeds[2], (FEATS,), jnp.float32, -3.140625, 3.140625), -3.140625, 3.140625),
        "sample_weight": draw_sample_weight(jax.random.fold_in(seeds[6], 71), 0),
        "stored": draw_stored(jax.random.fold_in(seeds[6], 71), 0),
        "root": jax.random.permutation(seeds[5], SLOTS).astype(jnp.int32),
    }


def make_features(inputs, freqs, phases, sample_weight):
    proj = jnp.dot(inputs, freqs, precision=lax.Precision.HIGHEST) + phases[None, :]
    return jnp.sqrt(sample_weight)[:, None] * jnp.cos(proj) / jnp.sqrt(jnp.float32(ROWS))

def reference(inputs, freqs, phases, sample_weight, stored, root):
    blocks_in = inputs.reshape(SLOTS, ROWS_DEV, IN_DIM)
    blocks_w = sample_weight.reshape(SLOTS, ROWS_DEV)

    def block_gram(pair):
        feats = make_features(pair[0], freqs, phases, pair[1])
        return jnp.dot(feats.T, feats, precision=lax.Precision.HIGHEST)

    def accumulate(total, pair):
        return (total + block_gram(pair), None)
    running = lax.dynamic_index_in_dim(stored, root[0].astype(jnp.int32), 0, keepdims=False)
    start = jnp.dot(running.T, running, precision=lax.Precision.HIGHEST)
    gram, unused = lax.scan(accumulate, start, (blocks_in, blocks_w))
    lower = jnp.linalg.cholesky(gram)
    factor = lower.T

    def block_basis(pair):
        feats = make_features(pair[0], freqs, phases, pair[1])
        solved = jax.scipy.linalg.solve_triangular(lower, feats.T, lower=True)
        return solved.T * jnp.sqrt(jnp.float32(ROWS))
    basis = lax.map(block_basis, (blocks_in, blocks_w)).reshape(ROWS, FEATS)
    return (factor, basis)
```

```python
import functools
import math

import jax
import jax.numpy as jnp
import numpy as np
from jax import lax
from jax.experimental import pallas as pl
from jax.experimental.pallas import tpu as pltpu
from jax.sharding import PartitionSpec as P

MESH = pl.DeviceIdType.MESH
HIGHEST = lax.Precision.HIGHEST
LANES = 128
BLOCK = 16
TILE_ROWS = 256

TWO_PI_HI = float(np.float32(round(2 * math.pi * 2**15) / 2**15))
TWO_PI_LO = float(np.float32(2 * math.pi - TWO_PI_HI))


def half_sine_coefs():
    top = (math.pi * 1.001) ** 2
    nodes = top * (0.5 + 0.5 * np.cos((np.arange(64) + 0.5) * math.pi / 64))
    roots = np.sqrt(nodes)
    values = math.sqrt(2.0) * np.sin(roots / 2) / roots
    fit = np.polynomial.chebyshev.Chebyshev.fit(nodes, values, 5, domain=[0, top])
    power = fit.convert(kind=np.polynomial.Polynomial)
    return [float(c) for c in power.coef]


COEFS = half_sine_coefs()


def cosine(x):
    turns = jnp.round(x * (1.0 / (2 * math.pi)))
    r = (x - turns * TWO_PI_HI) - turns * TWO_PI_LO
    t = r * r
    poly = jnp.full_like(t, COEFS[-1])
    for c in COEFS[-2::-1]:
        poly = poly * t + c
    s = r * poly
    return 1.0 - s * s


def local_gram(x_ref, freqs_ref, phases_ref, weight_ref, stored_ref, root_ref, feat, me, rows_all):
    rows, feats = feat.shape
    total = None
    mine = jnp.where(root_ref[0] == me, 1.0, 0.0).astype(jnp.float32)
    run = stored_ref[0] * mine
    total = lax.dot_general(run, run, (((0,), (0,)), ((), ())), precision=HIGHEST, preferred_element_type=jnp.float32)
    acc = None
    step = 256
    for at in range(0, rows, step):
        proj = lax.dot_general(
            x_ref[:, at : at + step], freqs_ref[...], (((0,), (0,)), ((), ())),
            precision=HIGHEST, preferred_element_type=jnp.float32,
        ) + phases_ref[...]
        scales = []
        for sub in range(step // LANES):
            row = jnp.sqrt(weight_ref[pl.ds(at // LANES + sub, 1), :])
            scales.append(jnp.broadcast_to(row, (LANES, LANES)).T)
        scale = jnp.concatenate(scales, axis=0)
        scale = jnp.concatenate([scale] * (feats // LANES), axis=1)
        block = cosine(proj) * scale
        feat[at : at + step, :] = block
        part = lax.dot_general(block, block, (((0,), (0,)), ((), ())), precision=HIGHEST, preferred_element_type=jnp.float32)
        acc = part if acc is None else acc + part
    return total + acc * (1.0 / rows_all)


def reduce_kernel(sizes, rows_all, x_ref, freqs_ref, phases_ref, weight_ref, stored_ref, root_ref,
                  gram_ref, feat_out, feat, mine, theirs, half, parts, zparts, back, last,
                  feat_sem, core_send, core_recv, rs_send, rs_recv, z_send, z_recv, ag_send, ag_recv, end_send, end_recv):
    nx, nz, ny = sizes
    grp, leaf = lax.axis_index("grp"), lax.axis_index("leaf")
    core, z, x = lax.rem(grp, 2), lax.rem(grp // 2, nz), grp // (2 * nz)

    def at(x_, z_, core_, y_):
        return ((x_ * nz + z_) * 2 + core_, y_)

    other = at(x, z, 1 - core, leaf)
    plane = []
    for dx in range(nx):
        for dy in range(ny):
            if dx or dy:
                plane.append((min(dx, nx - dx) + min(dy, ny - dy), dx, dy))
    plane.sort(key=lambda t: -t[0])
    plane = [(lax.rem(x + dx, nx), lax.rem(leaf + dy, ny)) for _, dx, dy in plane]
    line = sorted(range(1, nz), key=lambda d: -min(d, nz - d))
    line = [lax.rem(z + dz, nz) for dz in line]

    barrier = pltpu.get_barrier_semaphore()
    pl.semaphore_signal(barrier, inc=1, device_id=other, device_id_type=MESH)
    for px, py in plane:
        pl.semaphore_signal(barrier, inc=1, device_id=at(px, z, core, py), device_id_type=MESH)
    for pz in line:
        pl.semaphore_signal(barrier, inc=1, device_id=at(x, pz, core, leaf), device_id_type=MESH)

    me = grp * ny + leaf
    gram = local_gram(x_ref, freqs_ref, phases_ref, weight_ref, stored_ref, root_ref, feat, me, rows_all)
    feat_copy = pltpu.make_async_copy(feat, feat_out, feat_sem)
    feat_copy.start()
    feats = gram.shape[0]
    chunks = feats // 8
    for side in range(2):
        mine[side] = gram[:, side * LANES : (side + 1) * LANES].reshape(chunks, 8, LANES)

    pl.semaphore_wait(barrier, 1 + len(plane) + len(line))

    swap = pltpu.make_async_remote_copy(mine.at[1 - core], theirs, core_send, core_recv, device_id=other, device_id_type=MESH)
    swap.start()
    swap.wait_recv()
    half[...] = mine[core] + theirs[...]

    spot = x * ny + leaf
    copies = []
    for n, (px, py) in enumerate(plane):
        there = px * ny + py
        copies.append(pltpu.make_async_remote_copy(
            half.at[there], parts.at[n], rs_send.at[n], rs_recv.at[n],
            device_id=at(px, z, core, py), device_id_type=MESH))
    for c in copies:
        c.start()
    total = half[spot]
    for n in reversed(range(len(copies))):
        copies[n].wait_recv()
        total = total + parts[n]

    zparts[z] = total
    lines = []
    for n, pz in enumerate(line):
        lines.append(pltpu.make_async_remote_copy(
            zparts.at[z], zparts.at[z], z_send.at[n], z_recv.at[n],
            device_id=at(x, pz, core, leaf), device_id_type=MESH))
    for c in lines:
        c.start()
    for c in lines:
        c.wait_recv()
    total = zparts[0]
    for k in range(1, nz):
        total = total + zparts[k]

    back[spot] = total
    spread = []
    for n, (px, py) in enumerate(plane):
        spread.append(pltpu.make_async_remote_copy(
            back.at[spot], back.at[spot], ag_send.at[n], ag_recv.at[n],
            device_id=at(px, z, core, py), device_id_type=MESH))
    for c in spread:
        c.start()
    for c in spread:
        c.wait_recv()

    end = pltpu.make_async_remote_copy(back, last, end_send, end_recv, device_id=other, device_id_type=MESH)
    end.start()
    for c in [swap] + copies + lines + spread:
        c.wait_send()
    own = back[...].reshape(feats, LANES)
    end.wait_recv()
    got = last[...].reshape(feats, LANES)
    first = core == 0
    gram_ref[:, :LANES] = jnp.where(first, own, got)
    gram_ref[:, LANES:] = jnp.where(first, got, own)
    end.wait_send()
    feat_copy.wait()


def eliminate(a, factor_ref, inverse, block):
    n = a.shape[0]
    groups = block // 8
    sub8 = lax.broadcasted_iota(jnp.int32, (8, LANES), 0)
    rows_of = lax.broadcasted_iota(jnp.int32, (block, n), 0)
    cols_of = lax.broadcasted_iota(jnp.int32, (block, n), 1)
    ntile = n // LANES
    for r0 in range(0, n, block):
        panel = a[r0 : r0 + block, :]
        col = []
        for j in range(block):
            wide = jnp.broadcast_to(panel[:, r0 + j : r0 + j + 1], (block, LANES))
            col.append([wide[8 * g : 8 * g + 8] for g in range(groups)])
        base = (r0 // LANES) * LANES
        lane0 = r0 - base
        eye = (cols_of[:, :LANES] == rows_of[:, :LANES] + lane0).astype(jnp.float32)
        row = [[panel[8 * g : 8 * g + 8, LANES * t : LANES * t + LANES] for g in range(groups)] for t in range(ntile)]
        row.append([eye[8 * g : 8 * g + 8] for g in range(groups)])
        pivots = [None] * groups
        for k in range(block):
            gk, sk = divmod(k, 8)
            pivot = jnp.broadcast_to(col[k][gk][sk : sk + 1], (8, LANES))
            pivots[gk] = pivot if sk == 0 else jnp.where(sub8 >= sk, pivot, pivots[gk])
            if k == block - 1:
                break
            inv = 1.0 / pivot
            mult = {}
            for g in range(gk, groups):
                if g == gk and sk == 7:
                    continue
                m = col[k][g] * inv
                if g == gk:
                    m = jnp.where(sub8 > sk, m, 0.0)
                mult[g] = m
            for j in range(k + 1, block):
                lead = jnp.broadcast_to(col[j][gk][sk : sk + 1], (8, LANES))
                for g, m in mult.items():
                    col[j][g] = col[j][g] - m * lead
            for part in row:
                lead = jnp.broadcast_to(part[gk][sk : sk + 1], (8, LANES))
                for g, m in mult.items():
                    part[g] = part[g] - m * lead
        scale = [lax.rsqrt(p) for p in pivots]
        scaled = [jnp.concatenate([part[g] * scale[g] for g in range(groups)], axis=0) for part in row]
        full = jnp.concatenate(scaled[:ntile], axis=1)
        unit = jnp.concatenate([scaled[ntile]] * ntile, axis=1)
        upper = jnp.where(cols_of >= rows_of + r0, full, 0.0)
        factor_ref[r0 : r0 + block, :] = upper
        lower = jnp.where(cols_of < r0, full, jnp.where(cols_of <= rows_of + r0, unit, 0.0))
        inverse[r0 : r0 + block, :] = lower
        r1 = r0 + block
        if r1 < n:
            both = jnp.where(cols_of >= r1, full, lower)
            left = upper.T[r1:, :]
            drop = lax.dot_general(left, both, (((1,), (0,)), ((), ())), precision=HIGHEST, preferred_element_type=jnp.float32)
            old = a[r1:, :]
            cols_rest = lax.broadcasted_iota(jnp.int32, (n - r1, n), 1)
            fresh = (cols_rest >= r0) & (cols_rest < r1)
            a[r1:, :] = jnp.where(fresh, 0.0, old) - drop


def basis_kernel(gram_ref, feat_in, factor_ref, basis_out, a, inverse, feat, out, in_sem, out_sem):
    load = pltpu.make_async_copy(feat_in, feat, in_sem)
    load.start()
    a[...] = gram_ref[...]
    eliminate(a, factor_ref, inverse, BLOCK)
    right = inverse[...].T
    load.wait()
    rows = feat.shape[0]
    copies = []
    for n, at in enumerate(range(0, rows, TILE_ROWS)):
        tile = pl.ds(at, TILE_ROWS)
        out[tile, :] = jnp.dot(feat[tile, :], right, precision=HIGHEST, preferred_element_type=jnp.float32)
        c = pltpu.make_async_copy(out.at[tile, :], basis_out.at[tile, :], out_sem.at[n])
        c.start()
        copies.append(c)
    for c in copies:
        c.wait()


VMEM = functools.partial(pl.BlockSpec, memory_space=pltpu.VMEM)
ANY = functools.partial(pl.BlockSpec, memory_space=pl.ANY)


def run_basis(gram, features):
    rows, feats = features.shape
    f32 = jnp.float32
    return pl.pallas_call(
        basis_kernel,
        out_shape=(jax.ShapeDtypeStruct((feats, feats), f32), jax.ShapeDtypeStruct((rows, feats), f32)),
        in_specs=[VMEM(), ANY()],
        out_specs=(VMEM(), ANY()),
        scratch_shapes=[
            pltpu.VMEM((feats, feats), f32),
            pltpu.VMEM((feats, feats), f32),
            pltpu.VMEM((rows, feats), f32),
            pltpu.VMEM((rows, feats), f32),
            pltpu.SemaphoreType.DMA,
            pltpu.SemaphoreType.DMA((rows // TILE_ROWS,)),
        ],
        compiler_params=pltpu.CompilerParams(vmem_limit_bytes=32 * 2**20),
        name="basis",
    )(gram, features)


def per_device(sizes, rows_all, inputs, freqs, phases, sample_weight, stored, root):
    rows, feats = inputs.shape[0], freqs.shape[1]
    nx, nz, ny = sizes
    f32 = jnp.float32
    nplane, nline = nx * ny - 1, nz - 1
    chunks = feats // 8
    dma = pltpu.SemaphoreType.DMA
    gram, features = pl.pallas_call(
        functools.partial(reduce_kernel, sizes, rows_all),
        out_shape=(jax.ShapeDtypeStruct((feats, feats), f32), jax.ShapeDtypeStruct((rows, feats), f32)),
        in_specs=[VMEM()] * 5 + [pl.BlockSpec(memory_space=pltpu.SMEM)],
        out_specs=(VMEM(), ANY()),
        scratch_shapes=[
            pltpu.VMEM((rows, feats), f32),
            pltpu.VMEM((2, chunks, 8, LANES), f32),
            pltpu.VMEM((chunks, 8, LANES), f32),
            pltpu.VMEM((chunks, 8, LANES), f32),
            pltpu.VMEM((nplane, 8, LANES), f32),
            pltpu.VMEM((nz, 8, LANES), f32),
            pltpu.VMEM((chunks, 8, LANES), f32),
            pltpu.VMEM((chunks, 8, LANES), f32),
            dma, dma, dma,
            dma((nplane,)), dma((nplane,)),
            dma((nline,)), dma((nline,)),
            dma((nplane,)), dma((nplane,)),
            dma, dma,
        ],
        compiler_params=pltpu.CompilerParams(collective_id=0, has_side_effects=True, vmem_limit_bytes=32 * 2**20),
        name="reduce",
    )(inputs.T, freqs, phases[None, :], sample_weight.reshape(rows // LANES, LANES), stored, root)
    return run_basis(gram, features)


def solution(mesh):
    groups, leaves = mesh.shape["grp"], mesh.shape["leaf"]
    nx = 256 // 8 // leaves
    sizes = (nx, groups // 2 // nx, leaves)
    return jax.shard_map(
        lambda inputs, *rest: per_device(sizes, inputs.shape[0] * groups * leaves, inputs, *rest),
        mesh=mesh,
        in_specs=(
            P(("grp", "leaf"), None),
            P(),
            P(),
            P(("grp", "leaf")),
            P(("grp", "leaf"), None, None),
            P(),
        ),
        out_specs=(P(), P(("grp", "leaf"), None)),
        check_vma=False,
    )
```

```python
import functools
import math

import jax
import jax.numpy as jnp
import numpy as np
from jax import lax
from jax.experimental import pallas as pl
from jax.experimental.pallas import tpu as pltpu
from jax.sharding import PartitionSpec as P

MESH = pl.DeviceIdType.MESH
HIGHEST = lax.Precision.HIGHEST
LANES = 128
BLOCK = 16
TILE_ROWS = 256
STEP_ROWS = 512

TWO_PI_HI = float(np.float32(round(2 * math.pi * 2**15) / 2**15))
TWO_PI_LO = float(np.float32(2 * math.pi - TWO_PI_HI))


def half_sine_coefs():
    top = (math.pi * 1.001) ** 2
    nodes = top * (0.5 + 0.5 * np.cos((np.arange(64) + 0.5) * math.pi / 64))
    roots = np.sqrt(nodes)
    values = math.sqrt(2.0) * np.sin(roots / 2) / roots
    fit = np.polynomial.chebyshev.Chebyshev.fit(nodes, values, 5, domain=[0, top])
    power = fit.convert(kind=np.polynomial.Polynomial)
    return [float(c) for c in power.coef]


COEFS = half_sine_coefs()


def cosine(x):
    turns = jnp.round(x * (1.0 / (2 * math.pi)))
    r = (x - turns * TWO_PI_HI) - turns * TWO_PI_LO
    t = r * r
    poly = jnp.full_like(t, COEFS[-1])
    for c in COEFS[-2::-1]:
        poly = poly * t + c
    s = r * poly
    return 1.0 - s * s


def pieces(x):
    high = x.astype(jnp.bfloat16)
    rest = x - high.astype(jnp.float32)
    middle = rest.astype(jnp.bfloat16)
    return high, middle, (rest - middle.astype(jnp.float32)).astype(jnp.bfloat16)


def local_gram(x_ref, freqs_ref, phases_ref, weight_ref, stored_ref, root_ref, feat, me, rows_all):
    rows, feats = feat.shape
    down = (((0,), (0,)), ((), ()))
    high, middle, low = pieces(freqs_ref[...])
    freqs = jnp.concatenate([high, middle, high, middle, low, high], axis=0)
    acc = None
    for at in range(0, rows, STEP_ROWS):
        high, middle, low = pieces(x_ref[:, at : at + STEP_ROWS])
        x = jnp.concatenate([high, high, middle, middle, high, low], axis=0)
        proj = lax.dot_general(x, freqs, down, preferred_element_type=jnp.float32) + phases_ref[...]
        scales = []
        for sub in range(STEP_ROWS // LANES):
            row = jnp.sqrt(weight_ref[pl.ds(at // LANES + sub, 1), :])
            scales.append(jnp.broadcast_to(row, (LANES, LANES)).T)
        scale = jnp.concatenate(scales, axis=0)
        scale = jnp.concatenate([scale] * (feats // LANES), axis=1)
        block = cosine(proj) * scale
        feat[at : at + STEP_ROWS, :] = block
        part = lax.dot_general(block, block, down, precision=HIGHEST, preferred_element_type=jnp.float32)
        acc = part if acc is None else acc + part
    run = stored_ref[0] * jnp.where(root_ref[0] == me, 1.0, 0.0).astype(jnp.float32)
    running = lax.dot_general(run, run, down, precision=HIGHEST, preferred_element_type=jnp.float32)
    return running + acc * (1.0 / rows_all)


def reduce_kernel(sizes, rows_all, *refs):
    sources, refs = refs[:6], refs[6:]
    loaded, load_sem, refs = refs[2:8], refs[8], refs[:2] + refs[9:]
    loads = [pltpu.make_async_copy(s, d, load_sem.at[n]) for n, (s, d) in enumerate(zip(sources, loaded))]
    for c in loads:
        c.start()
    reduce_loaded(sizes, rows_all, loads, *loaded, *refs)


def reduce_loaded(sizes, rows_all, loads, x_ref, freqs_ref, phases_ref, weight_ref, stored_ref, root_ref,
                  gram_out, feat_out, feat, mine, theirs, half, parts, zparts, back,
                  feat_sem, core_send, core_recv, rs_send, rs_recv, z_send, z_recv, ag_send, ag_recv, end_send, end_recv, keep_sem):
    nx, nz, ny = sizes
    grp, leaf = lax.axis_index("grp"), lax.axis_index("leaf")
    core, z, x = lax.rem(grp, 2), lax.rem(grp // 2, nz), grp // (2 * nz)

    def at(x_, z_, core_, y_):
        return ((x_ * nz + z_) * 2 + core_, y_)

    other = at(x, z, 1 - core, leaf)
    plane = []
    for dx in range(nx):
        for dy in range(ny):
            if dx or dy:
                plane.append((min(dx, nx - dx) + min(dy, ny - dy), dx, dy))
    plane.sort(key=lambda t: -t[0])
    plane = [(lax.rem(x + dx, nx), lax.rem(leaf + dy, ny)) for _, dx, dy in plane]
    line = sorted(range(1, nz), key=lambda d: -min(d, nz - d))
    line = [lax.rem(z + dz, nz) for dz in line]

    barrier = pltpu.get_barrier_semaphore()
    pl.semaphore_signal(barrier, inc=1, device_id=other, device_id_type=MESH)
    for px, py in plane:
        pl.semaphore_signal(barrier, inc=1, device_id=at(px, z, core, py), device_id_type=MESH)
    for pz in line:
        pl.semaphore_signal(barrier, inc=1, device_id=at(x, pz, core, leaf), device_id_type=MESH)

    me = grp * ny + leaf
    for c in loads:
        c.wait()
    gram = local_gram(x_ref, freqs_ref, phases_ref, weight_ref, stored_ref, root_ref, feat, me, rows_all)
    feat_copy = pltpu.make_async_copy(feat, feat_out, feat_sem)
    feat_copy.start()
    feats = gram.shape[0]
    chunks = feats // 8
    for side in range(2):
        mine[side] = gram[:, side * LANES : (side + 1) * LANES].reshape(chunks, 8, LANES)

    pl.semaphore_wait(barrier, 1 + len(plane) + len(line))

    swap = pltpu.make_async_remote_copy(mine.at[1 - core], theirs, core_send, core_recv, device_id=other, device_id_type=MESH)
    swap.start()
    swap.wait_recv()
    half[...] = mine[core] + theirs[...]

    spot = x * ny + leaf
    copies = []
    for n, (px, py) in enumerate(plane):
        there = px * ny + py
        copies.append(pltpu.make_async_remote_copy(
            half.at[there], parts.at[n], rs_send.at[n], rs_recv.at[n],
            device_id=at(px, z, core, py), device_id_type=MESH))
    for c in copies:
        c.start()
    total = half[spot]
    for n in reversed(range(len(copies))):
        copies[n].wait_recv()
        total = total + parts[n]

    zparts[z] = total
    lines = []
    for n, pz in enumerate(line):
        lines.append(pltpu.make_async_remote_copy(
            zparts.at[z], zparts.at[z], z_send.at[n], z_recv.at[n],
            device_id=at(x, pz, core, leaf), device_id_type=MESH))
    for c in lines:
        c.start()
    for c in lines:
        c.wait_recv()
    total = zparts[0]
    for k in range(1, nz):
        total = total + zparts[k]

    back[spot] = total
    spread = []
    for n, (px, py) in enumerate(plane):
        spread.append(pltpu.make_async_remote_copy(
            back.at[spot], back.at[spot], ag_send.at[n], ag_recv.at[n],
            device_id=at(px, z, core, py), device_id_type=MESH))
    for c in spread:
        c.start()
    for c in spread:
        c.wait_recv()

    end = pltpu.make_async_remote_copy(back, gram_out.at[core], end_send, end_recv, device_id=other, device_id_type=MESH)
    end.start()
    keep = pltpu.make_async_copy(back, gram_out.at[core], keep_sem)
    keep.start()
    for c in [swap] + copies + lines + spread:
        c.wait_send()
    feat_copy.wait()
    keep.wait()
    end.wait()


def columns(values, first, block):
    out = []
    for j in range(block):
        wide = jnp.broadcast_to(values[:, first + j : first + j + 1], (block, LANES))
        out.append([wide[8 * g : 8 * g + 8] for g in range(block // 8)])
    return out


def eliminate(a, factor, inverse, block):
    n = a.shape[0]
    groups = block // 8
    ntile = n // LANES
    sub8 = lax.broadcasted_iota(jnp.int32, (8, LANES), 0)
    rows_of = lax.broadcasted_iota(jnp.int32, (block, n), 0)
    cols_of = lax.broadcasted_iota(jnp.int32, (block, n), 1)

    def spread(part, g, s):
        return jnp.broadcast_to(part[g][s : s + 1], (8, LANES))

    def split(values):
        return [[values[8 * g : 8 * g + 8, LANES * t : LANES * t + LANES] for g in range(groups)] for t in range(values.shape[1] // LANES)]

    def within(cols, lo):
        return (cols >= lo) & (cols < lo + block)

    panel = a[0:block, :]
    drop = None
    for r0 in range(0, n, block):
        r1, r2 = r0 + block, r0 + 2 * block
        ahead = r1 < n
        col = columns(panel, r0, block)
        if ahead:
            base = (r1 // LANES) * LANES
            turned = panel[:, base : base + LANES].T[r1 - base : r2 - base, :]
            below = columns(turned, 0, block)
        lane0 = r0 % LANES
        eye = (cols_of[:, :LANES] == rows_of[:, :LANES] + lane0).astype(jnp.float32)
        row = split(panel) + split(eye)
        gone = [[None] * groups for _ in row]
        pivots = [None] * groups
        for k in range(block):
            gk, sk = divmod(k, 8)
            pivot = spread(col[k], gk, sk)
            pivots[gk] = pivot if sk == 0 else jnp.where(sub8 >= sk, pivot, pivots[gk])
            inv = 1.0 / pivot
            mult = {}
            for g in range(gk, groups):
                if g == gk and sk == 7:
                    continue
                m = col[k][g] * inv
                if g == gk:
                    m = jnp.where(sub8 > sk, m, 0.0)
                mult[g] = m
            under = [below[k][g] * inv for g in range(groups)] if ahead else []
            for j in range(k + 1, block):
                lead = spread(col[j], gk, sk)
                for g, m in mult.items():
                    col[j][g] = col[j][g] - m * lead
                for g, m in enumerate(under):
                    below[j][g] = below[j][g] - m * lead
            for part, taken in zip(row, gone):
                lead = spread(part, gk, sk)
                for g, m in mult.items():
                    part[g] = part[g] - m * lead
                for g, m in enumerate(under):
                    taken[g] = m * lead if k == 0 else taken[g] + m * lead
        scale = [lax.rsqrt(p) for p in pivots]
        scaled = [jnp.concatenate([part[g] * scale[g] for g in range(groups)], axis=0) for part in row]
        full = jnp.concatenate(scaled[:ntile], axis=1)
        unit = jnp.concatenate([scaled[ntile]] * ntile, axis=1)
        upper = jnp.where(cols_of >= rows_of + r0, full, 0.0)
        factor[r0:r1, :] = upper
        lower = jnp.where(cols_of < r0, full, jnp.where(cols_of <= rows_of + r0, unit, 0.0))
        inverse[r0:r1, :] = lower
        if drop is not None and ahead:
            cols_rest = lax.broadcasted_iota(jnp.int32, (n - r1, n), 1)
            a[r1:, :] = jnp.where(within(cols_rest, r0 - block), 0.0, a[r1:, :]) - drop
        if r2 < n:
            both = jnp.where(cols_of >= r1, full, lower)
            left = upper.T[r2:, :]
            drop = lax.dot_general(left, both, (((1,), (0,)), ((), ())), precision=HIGHEST, preferred_element_type=jnp.float32)
        if ahead:
            taken = [jnp.concatenate(part, axis=0) for part in gone]
            rest = jnp.concatenate(taken[:ntile], axis=1)
            own = jnp.concatenate([taken[ntile]] * ntile, axis=1)
            here = within(cols_of, r0)
            panel = jnp.where(here, 0.0, a[r1:r2, :]) - jnp.where(here, own, rest)


def basis_kernel(gram_in, feat_in, factor_out, basis_out, gram, a, factor, inverse, feat, out, in_sem, factor_sem, out_sem):
    first = pltpu.make_async_copy(gram_in, gram, in_sem.at[0])
    first.start()
    load = pltpu.make_async_copy(feat_in, feat, in_sem.at[1])
    load.start()
    first.wait()
    feats = a.shape[0]
    for side in range(2):
        a[:, side * LANES : (side + 1) * LANES] = gram[side].reshape(feats, LANES)
    eliminate(a, factor, inverse, BLOCK)
    copies = [pltpu.make_async_copy(factor, factor_out, factor_sem)]
    copies[0].start()
    right = inverse[...].T
    load.wait()
    rows = feat.shape[0]
    for n, at in enumerate(range(0, rows, TILE_ROWS)):
        tile = pl.ds(at, TILE_ROWS)
        out[tile, :] = jnp.dot(feat[tile, :], right, precision=HIGHEST, preferred_element_type=jnp.float32)
        c = pltpu.make_async_copy(out.at[tile, :], basis_out.at[tile, :], out_sem.at[n])
        c.start()
        copies.append(c)
    for c in copies:
        c.wait()


VMEM = functools.partial(pl.BlockSpec, memory_space=pltpu.VMEM)
HBM = functools.partial(pl.BlockSpec, memory_space=pltpu.HBM)


def run_basis(gram, features):
    rows, feats = features.shape
    f32 = jnp.float32
    square = pltpu.VMEM((feats, feats), f32)
    return pl.pallas_call(
        basis_kernel,
        out_shape=(jax.ShapeDtypeStruct((feats, feats), f32), jax.ShapeDtypeStruct((rows, feats), f32)),
        in_specs=[HBM(), HBM()],
        out_specs=(HBM(), HBM()),
        scratch_shapes=[
            pltpu.VMEM(gram.shape, f32),
            square, square, square,
            pltpu.VMEM((rows, feats), f32),
            pltpu.VMEM((rows, feats), f32),
            pltpu.SemaphoreType.DMA((2,)),
            pltpu.SemaphoreType.DMA,
            pltpu.SemaphoreType.DMA((rows // TILE_ROWS,)),
        ],
        compiler_params=pltpu.CompilerParams(vmem_limit_bytes=60 * 2**20),
        name="basis",
    )(gram, features)


def per_device(sizes, rows_all, inputs, freqs, phases, sample_weight, stored, root):
    rows, feats = inputs.shape[0], freqs.shape[1]
    nx, nz, ny = sizes
    f32 = jnp.float32
    nplane, nline = nx * ny - 1, nz - 1
    chunks = feats // 8
    dma = pltpu.SemaphoreType.DMA
    gram, features = pl.pallas_call(
        functools.partial(reduce_kernel, sizes, rows_all),
        out_shape=(jax.ShapeDtypeStruct((2, chunks, 8, LANES), f32), jax.ShapeDtypeStruct((rows, feats), f32)),
        in_specs=[HBM()] * 6,
        out_specs=(HBM(), HBM()),
        scratch_shapes=[
            pltpu.VMEM((inputs.shape[1], rows), f32),
            pltpu.VMEM(freqs.shape, f32),
            pltpu.VMEM((1, feats), f32),
            pltpu.VMEM((rows // LANES, LANES), f32),
            pltpu.VMEM(stored.shape, f32),
            pltpu.SMEM(root.shape, jnp.int32),
            dma((6,)),
            pltpu.VMEM((rows, feats), f32),
            pltpu.VMEM((2, chunks, 8, LANES), f32),
            pltpu.VMEM((chunks, 8, LANES), f32),
            pltpu.VMEM((chunks, 8, LANES), f32),
            pltpu.VMEM((nplane, 8, LANES), f32),
            pltpu.VMEM((nz, 8, LANES), f32),
            pltpu.VMEM((chunks, 8, LANES), f32),
            dma, dma, dma,
            dma((nplane,)), dma((nplane,)),
            dma((nline,)), dma((nline,)),
            dma((nplane,)), dma((nplane,)),
            dma, dma, dma,
        ],
        compiler_params=pltpu.CompilerParams(collective_id=0, has_side_effects=True, vmem_limit_bytes=60 * 2**20),
        name="reduce",
    )(inputs.T, freqs, phases[None, :], sample_weight.reshape(rows // LANES, LANES), stored, root)
    return run_basis(gram, features)


def solution(mesh):
    groups, leaves = mesh.shape["grp"], mesh.shape["leaf"]
    nx = 256 // 8 // leaves
    sizes = (nx, groups // 2 // nx, leaves)
    return jax.shard_map(
        lambda inputs, *rest: per_device(sizes, inputs.shape[0] * groups * leaves, inputs, *rest),
        mesh=mesh,
        in_specs=(
            P(("grp", "leaf"), None),
            P(),
            P(),
            P(("grp", "leaf")),
            P(("grp", "leaf"), None, None),
            P(),
        ),
        out_specs=(P(), P(("grp", "leaf"), None)),
        check_vma=False,
    )
```

```python
import functools
import math

import jax
import jax.numpy as jnp
import numpy as np
from jax import lax
from jax.experimental import pallas as pl
from jax.experimental.pallas import tpu as pltpu
from jax.sharding import PartitionSpec as P

MESH = pl.DeviceIdType.MESH
HIGHEST = lax.Precision.HIGHEST
LANES = 128
BLOCK = 16
TILE_ROWS = 256
STEP_ROWS = 1024
CHUNK_ROWS = 5

TWO_PI_HI = float(np.float32(round(2 * math.pi * 2**15) / 2**15))
TWO_PI_LO = float(np.float32(2 * math.pi - TWO_PI_HI))


def half_sine_coefs():
    top = (math.pi * 1.001) ** 2
    nodes = top * (0.5 + 0.5 * np.cos((np.arange(64) + 0.5) * math.pi / 64))
    roots = np.sqrt(nodes)
    values = math.sqrt(2.0) * np.sin(roots / 2) / roots
    fit = np.polynomial.chebyshev.Chebyshev.fit(nodes, values, 5, domain=[0, top])
    power = fit.convert(kind=np.polynomial.Polynomial)
    return [float(c) for c in power.coef]


COEFS = half_sine_coefs()


def cosine(x):
    turns = jnp.round(x * (1.0 / (2 * math.pi)))
    r = (x - turns * TWO_PI_HI) - turns * TWO_PI_LO
    t = r * r
    poly = jnp.full_like(t, COEFS[-1])
    for c in COEFS[-2::-1]:
        poly = poly * t + c
    s = r * poly
    return 1.0 - s * s


def pieces(x):
    high = x.astype(jnp.bfloat16)
    rest = x - high.astype(jnp.float32)
    middle = rest.astype(jnp.bfloat16)
    return high, middle, (rest - middle.astype(jnp.float32)).astype(jnp.bfloat16)


def local_gram(x_ref, freqs_ref, phases_ref, weight_ref, stored_ref, root_ref, feat, me, rows_all):
    rows, feats = feat.shape
    down = (((0,), (0,)), ((), ()))
    high, middle, low = pieces(freqs_ref[...])
    freqs = jnp.concatenate([high, middle, high, middle, low, high], axis=0)
    acc = None
    for at in range(0, rows, STEP_ROWS):
        high, middle, low = pieces(x_ref[:, at : at + STEP_ROWS])
        x = jnp.concatenate([high, high, middle, middle, high, low], axis=0)
        proj = lax.dot_general(x, freqs, down, preferred_element_type=jnp.float32) + phases_ref[...]
        scales = []
        for sub in range(STEP_ROWS // LANES):
            row = jnp.sqrt(weight_ref[pl.ds(at // LANES + sub, 1), :])
            scales.append(jnp.broadcast_to(row, (LANES, LANES)).T)
        scale = jnp.concatenate(scales, axis=0)
        scale = jnp.concatenate([scale] * (feats // LANES), axis=1)
        block = cosine(proj) * scale
        feat[at : at + STEP_ROWS, :] = block
        high, middle, low = pieces(block)
        part = lax.dot_general(high, jnp.concatenate([high, middle, low], axis=1), down, preferred_element_type=jnp.float32)
        cross = part[:, feats : 2 * feats] + part[:, 2 * feats :]
        even = part[:, :feats] + lax.dot_general(middle, middle, down, preferred_element_type=jnp.float32)
        acc = (even, cross) if acc is None else (acc[0] + even, acc[1] + cross)
    run = stored_ref[0] * jnp.where(root_ref[0] == me, 1.0, 0.0).astype(jnp.float32)
    running = lax.dot_general(run, run, down, precision=HIGHEST, preferred_element_type=jnp.float32)
    return running + (acc[0] + (acc[1] + acc[1].T)) * (1.0 / rows_all)


def triangles():
    row = lax.broadcasted_iota(jnp.int32, (LANES, LANES), 0)
    col = lax.broadcasted_iota(jnp.int32, (LANES, LANES), 1)
    return row, col


def pack(gram, mine):
    row, col = triangles()
    last = gram[LANES:, LANES:]
    squares = [jnp.where(row <= col, gram[:LANES, :LANES], last), gram[:LANES, LANES:]]
    diagonal = jnp.sum(jnp.where(row == col, last, 0.0), axis=0, keepdims=True)
    for side, square in enumerate(squares):
        for n in range(LANES // 4):
            mine[side, n, 0:4, :] = square[4 * n : 4 * n + 4]
            if side or n:
                mine[side, n, 4:5, :] = jnp.zeros((1, LANES), jnp.float32)
    mine[0, 0, 4:5, :] = diagonal


def unpack(chunks, a):
    row, col = triangles()
    squares = [jnp.concatenate([chunks[side, n, 0:4, :] for n in range(LANES // 4)], axis=0) for side in range(2)]
    mixed = squares[0]
    turned = mixed.T
    a[:LANES, :LANES] = jnp.where(row <= col, mixed, turned)
    a[:LANES, LANES:] = squares[1]
    a[LANES:, :LANES] = jnp.zeros((LANES, LANES), jnp.float32)
    a[LANES:, LANES:] = jnp.where(row > col, mixed, jnp.where(row < col, turned, chunks[0, 0, 4:5, :]))


def reduce_kernel(sizes, rows_all, *refs):
    sources, refs = refs[:6], refs[6:]
    loaded, load_sem, refs = refs[2:8], refs[8], refs[:2] + refs[9:]
    loads = [pltpu.make_async_copy(s, d, load_sem.at[n]) for n, (s, d) in enumerate(zip(sources, loaded))]
    for c in loads:
        c.start()
    reduce_loaded(sizes, rows_all, loads, *loaded, *refs)


def reduce_loaded(sizes, rows_all, loads, x_ref, freqs_ref, phases_ref, weight_ref, stored_ref, root_ref,
                  gram_out, feat_out, feat, mine, theirs, half, parts, zparts, back,
                  feat_sem, core_send, core_recv, rs_send, rs_recv, z_send, z_recv, ag_send, ag_recv, end_send, end_recv, keep_sem):
    nx, nz, ny = sizes
    grp, leaf = lax.axis_index("grp"), lax.axis_index("leaf")
    core, z, x = lax.rem(grp, 2), lax.rem(grp // 2, nz), grp // (2 * nz)

    def at(x_, z_, core_, y_):
        return ((x_ * nz + z_) * 2 + core_, y_)

    other = at(x, z, 1 - core, leaf)
    plane = []
    for dx in range(nx):
        for dy in range(ny):
            if dx or dy:
                plane.append((min(dx, nx - dx) + min(dy, ny - dy), dx, dy))
    plane.sort(key=lambda t: -t[0])
    plane = [(lax.rem(x + dx, nx), lax.rem(leaf + dy, ny)) for _, dx, dy in plane]
    line = sorted(range(1, nz), key=lambda d: -min(d, nz - d))
    line = [lax.rem(z + dz, nz) for dz in line]

    barrier = pltpu.get_barrier_semaphore()
    pl.semaphore_signal(barrier, inc=1, device_id=other, device_id_type=MESH)
    for px, py in plane:
        pl.semaphore_signal(barrier, inc=1, device_id=at(px, z, core, py), device_id_type=MESH)
    for pz in line:
        pl.semaphore_signal(barrier, inc=1, device_id=at(x, pz, core, leaf), device_id_type=MESH)

    me = grp * ny + leaf
    for c in loads:
        c.wait()
    gram = local_gram(x_ref, freqs_ref, phases_ref, weight_ref, stored_ref, root_ref, feat, me, rows_all)
    feat_copy = pltpu.make_async_copy(feat, feat_out, feat_sem)
    feat_copy.start()
    pack(gram, mine)

    pl.semaphore_wait(barrier, 1 + len(plane) + len(line))

    swap = pltpu.make_async_remote_copy(mine.at[1 - core], theirs, core_send, core_recv, device_id=other, device_id_type=MESH)
    swap.start()
    swap.wait_recv()
    half[...] = mine[core] + theirs[...]

    spot = x * ny + leaf
    copies = []
    for n, (px, py) in enumerate(plane):
        there = px * ny + py
        copies.append(pltpu.make_async_remote_copy(
            half.at[there], parts.at[n], rs_send.at[n], rs_recv.at[n],
            device_id=at(px, z, core, py), device_id_type=MESH))
    for c in copies:
        c.start()
    total = half[spot]
    for n in reversed(range(len(copies))):
        copies[n].wait_recv()
        total = total + parts[n]

    zparts[z] = total
    lines = []
    for n, pz in enumerate(line):
        lines.append(pltpu.make_async_remote_copy(
            zparts.at[z], zparts.at[z], z_send.at[n], z_recv.at[n],
            device_id=at(x, pz, core, leaf), device_id_type=MESH))
    for c in lines:
        c.start()
    for c in lines:
        c.wait_recv()
    total = zparts[0]
    for k in range(1, nz):
        total = total + zparts[k]

    back[spot] = total
    spread = []
    for n, (px, py) in enumerate(plane):
        spread.append(pltpu.make_async_remote_copy(
            back.at[spot], back.at[spot], ag_send.at[n], ag_recv.at[n],
            device_id=at(px, z, core, py), device_id_type=MESH))
    for c in spread:
        c.start()
    for c in spread:
        c.wait_recv()

    end = pltpu.make_async_remote_copy(back, gram_out.at[core], end_send, end_recv, device_id=other, device_id_type=MESH)
    end.start()
    keep = pltpu.make_async_copy(back, gram_out.at[core], keep_sem)
    keep.start()
    for c in [swap] + copies + lines + spread:
        c.wait_send()
    feat_copy.wait()
    keep.wait()
    end.wait()


def columns(values, first, block):
    out = []
    for j in range(block):
        wide = jnp.broadcast_to(values[:, first + j : first + j + 1], (block, LANES))
        out.append([wide[8 * g : 8 * g + 8] for g in range(block // 8)])
    return out


def eliminate(a, factor, inverse, block):
    n = a.shape[0]
    groups = block // 8
    ntile = n // LANES
    sub8 = lax.broadcasted_iota(jnp.int32, (8, LANES), 0)
    rows_of = lax.broadcasted_iota(jnp.int32, (block, n), 0)
    cols_of = lax.broadcasted_iota(jnp.int32, (block, n), 1)

    def spread(part, g, s):
        return jnp.broadcast_to(part[g][s : s + 1], (8, LANES))

    def split(values):
        return [[values[8 * g : 8 * g + 8, LANES * t : LANES * t + LANES] for g in range(groups)] for t in range(values.shape[1] // LANES)]

    def within(cols, lo):
        return (cols >= lo) & (cols < lo + block)

    panel = a[0:block, :]
    drop = None
    for r0 in range(0, n, block):
        r1, r2 = r0 + block, r0 + 2 * block
        ahead = r1 < n
        col = columns(panel, r0, block)
        if ahead:
            base = (r1 // LANES) * LANES
            turned = panel[:, base : base + LANES].T[r1 - base : r2 - base, :]
            below = columns(turned, 0, block)
        lane0 = r0 % LANES
        eye = (cols_of[:, :LANES] == rows_of[:, :LANES] + lane0).astype(jnp.float32)
        row = split(panel) + split(eye)
        gone = [[None] * groups for _ in row]
        pivots = [None] * groups
        for k in range(block):
            gk, sk = divmod(k, 8)
            pivot = spread(col[0], 0, 0) if k == 0 else coming
            pivots[gk] = pivot if sk == 0 else jnp.where(sub8 >= sk, pivot, pivots[gk])
            inv = 1.0 / pivot
            if k + 1 < block:
                gn, sn = divmod(k + 1, 8)
                coming = spread(col[k + 1], gn, sn) - (spread(col[k], gn, sn) * spread(col[k + 1], gk, sk)) * inv
            mult = {}
            for g in range(gk, groups):
                if g == gk and sk == 7:
                    continue
                m = col[k][g] * inv
                if g == gk:
                    m = jnp.where(sub8 > sk, m, 0.0)
                mult[g] = m
            under = [below[k][g] * inv for g in range(groups)] if ahead else []
            for j in range(k + 1, block):
                lead = spread(col[j], gk, sk)
                for g, m in mult.items():
                    col[j][g] = col[j][g] - m * lead
                for g, m in enumerate(under):
                    below[j][g] = below[j][g] - m * lead
            for part, taken in zip(row, gone):
                lead = spread(part, gk, sk)
                for g, m in mult.items():
                    part[g] = part[g] - m * lead
                for g, m in enumerate(under):
                    taken[g] = m * lead if k == 0 else taken[g] + m * lead
        scale = [lax.rsqrt(p) for p in pivots]
        scaled = [jnp.concatenate([part[g] * scale[g] for g in range(groups)], axis=0) for part in row]
        full = jnp.concatenate(scaled[:ntile], axis=1)
        unit = jnp.concatenate([scaled[ntile]] * ntile, axis=1)
        upper = jnp.where(cols_of >= rows_of + r0, full, 0.0)
        factor[r0:r1, :] = upper
        lower = jnp.where(cols_of < r0, full, jnp.where(cols_of <= rows_of + r0, unit, 0.0))
        inverse[r0:r1, :] = lower
        if drop is not None and ahead:
            cols_rest = lax.broadcasted_iota(jnp.int32, (n - r1, n), 1)
            a[r1:, :] = jnp.where(within(cols_rest, r0 - block), 0.0, a[r1:, :]) - drop
        if r2 < n:
            both = jnp.where(cols_of >= r1, full, lower)
            left = upper.T[r2:, :]
            drop = lax.dot_general(left, both, (((1,), (0,)), ((), ())), precision=HIGHEST, preferred_element_type=jnp.float32)
        if ahead:
            taken = [jnp.concatenate(part, axis=0) for part in gone]
            rest = jnp.concatenate(taken[:ntile], axis=1)
            own = jnp.concatenate([taken[ntile]] * ntile, axis=1)
            here = within(cols_of, r0)
            panel = jnp.where(here, 0.0, a[r1:r2, :]) - jnp.where(here, own, rest)


def basis_kernel(gram_in, feat_in, factor_out, basis_out, gram, a, factor, inverse, feat, out, in_sem, factor_sem, out_sem):
    first = pltpu.make_async_copy(gram_in, gram, in_sem.at[0])
    first.start()
    load = pltpu.make_async_copy(feat_in, feat, in_sem.at[1])
    load.start()
    first.wait()
    unpack(gram, a)
    eliminate(a, factor, inverse, BLOCK)
    copies = [pltpu.make_async_copy(factor, factor_out, factor_sem)]
    copies[0].start()
    right = inverse[...].T
    load.wait()
    rows = feat.shape[0]
    for n, at in enumerate(range(0, rows, TILE_ROWS)):
        tile = pl.ds(at, TILE_ROWS)
        out[tile, :] = jnp.dot(feat[tile, :], right, precision=HIGHEST, preferred_element_type=jnp.float32)
        c = pltpu.make_async_copy(out.at[tile, :], basis_out.at[tile, :], out_sem.at[n])
        c.start()
        copies.append(c)
    for c in copies:
        c.wait()


VMEM = functools.partial(pl.BlockSpec, memory_space=pltpu.VMEM)
HBM = functools.partial(pl.BlockSpec, memory_space=pltpu.HBM)


def run_basis(gram, features):
    rows, feats = features.shape
    f32 = jnp.float32
    square = pltpu.VMEM((feats, feats), f32)
    return pl.pallas_call(
        basis_kernel,
        out_shape=(jax.ShapeDtypeStruct((feats, feats), f32), jax.ShapeDtypeStruct((rows, feats), f32)),
        in_specs=[HBM(), HBM()],
        out_specs=(HBM(), HBM()),
        scratch_shapes=[
            pltpu.VMEM(gram.shape, f32),
            square, square, square,
            pltpu.VMEM((rows, feats), f32),
            pltpu.VMEM((rows, feats), f32),
            pltpu.SemaphoreType.DMA((2,)),
            pltpu.SemaphoreType.DMA,
            pltpu.SemaphoreType.DMA((rows // TILE_ROWS,)),
        ],
        compiler_params=pltpu.CompilerParams(vmem_limit_bytes=60 * 2**20),
        name="basis",
    )(gram, features)


def per_device(sizes, rows_all, inputs, freqs, phases, sample_weight, stored, root):
    rows, feats = inputs.shape[0], freqs.shape[1]
    nx, nz, ny = sizes
    f32 = jnp.float32
    nplane, nline = nx * ny - 1, nz - 1
    chunks = LANES // 4
    dma = pltpu.SemaphoreType.DMA
    gram, features = pl.pallas_call(
        functools.partial(reduce_kernel, sizes, rows_all),
        out_shape=(jax.ShapeDtypeStruct((2, chunks, CHUNK_ROWS, LANES), f32), jax.ShapeDtypeStruct((rows, feats), f32)),
        in_specs=[HBM()] * 6,
        out_specs=(HBM(), HBM()),
        scratch_shapes=[
            pltpu.VMEM((inputs.shape[1], rows), f32),
            pltpu.VMEM(freqs.shape, f32),
            pltpu.VMEM((1, feats), f32),
            pltpu.VMEM((rows // LANES, LANES), f32),
            pltpu.VMEM(stored.shape, f32),
            pltpu.SMEM(root.shape, jnp.int32),
            dma((6,)),
            pltpu.VMEM((rows, feats), f32),
            pltpu.VMEM((2, chunks, CHUNK_ROWS, LANES), f32),
            pltpu.VMEM((chunks, CHUNK_ROWS, LANES), f32),
            pltpu.VMEM((chunks, CHUNK_ROWS, LANES), f32),
            pltpu.VMEM((nplane, CHUNK_ROWS, LANES), f32),
            pltpu.VMEM((nz, CHUNK_ROWS, LANES), f32),
            pltpu.VMEM((chunks, CHUNK_ROWS, LANES), f32),
            dma, dma, dma,
            dma((nplane,)), dma((nplane,)),
            dma((nline,)), dma((nline,)),
            dma((nplane,)), dma((nplane,)),
            dma, dma, dma,
        ],
        compiler_params=pltpu.CompilerParams(collective_id=0, has_side_effects=True, vmem_limit_bytes=60 * 2**20),
        name="reduce",
    )(inputs.T, freqs, phases[None, :], sample_weight.reshape(rows // LANES, LANES), stored, root)
    return run_basis(gram, features)


def solution(mesh):
    groups, leaves = mesh.shape["grp"], mesh.shape["leaf"]
    nx = LANES // 4 // leaves
    sizes = (nx, groups // 2 // nx, leaves)
    return jax.shard_map(
        lambda inputs, *rest: per_device(sizes, inputs.shape[0] * groups * leaves, inputs, *rest),
        mesh=mesh,
        in_specs=(
            P(("grp", "leaf"), None),
            P(),
            P(),
            P(("grp", "leaf")),
            P(("grp", "leaf"), None, None),
            P(),
        ),
        out_specs=(P(), P(("grp", "leaf"), None)),
        check_vma=False,
    )
```

```python
import functools
import math

import jax
import jax.numpy as jnp
import numpy as np
from jax import lax
from jax.experimental import pallas as pl
from jax.experimental.pallas import tpu as pltpu
from jax.sharding import PartitionSpec as P

MESH = pl.DeviceIdType.MESH
HIGHEST = lax.Precision.HIGHEST
LANES = 128
BLOCK = 16
TILE_ROWS = 256
STEP_ROWS = 1024
CHUNK_ROWS = 5

TWO_PI_HI = float(np.float32(round(2 * math.pi * 2**15) / 2**15))
TWO_PI_LO = float(np.float32(2 * math.pi - TWO_PI_HI))


def half_sine_coefs():
    top = (math.pi * 1.001) ** 2
    nodes = top * (0.5 + 0.5 * np.cos((np.arange(64) + 0.5) * math.pi / 64))
    roots = np.sqrt(nodes)
    values = math.sqrt(2.0) * np.sin(roots / 2) / roots
    fit = np.polynomial.chebyshev.Chebyshev.fit(nodes, values, 4, domain=[0, top])
    power = fit.convert(kind=np.polynomial.Polynomial)
    return [float(c) for c in power.coef]


COEFS = half_sine_coefs()


def cosine(x):
    turns = jnp.round(x * (1.0 / (2 * math.pi)))
    r = (x - turns * TWO_PI_HI) - turns * TWO_PI_LO
    t = r * r
    poly = jnp.full_like(t, COEFS[-1])
    for c in COEFS[-2::-1]:
        poly = poly * t + c
    s = r * poly
    return 1.0 - s * s


def pieces(x):
    high = x.astype(jnp.bfloat16)
    rest = x - high.astype(jnp.float32)
    middle = rest.astype(jnp.bfloat16)
    return high, middle, (rest - middle.astype(jnp.float32)).astype(jnp.bfloat16)


def local_gram(x_ref, freqs_ref, phases_ref, weight_ref, stored_ref, root_ref, feat, me, rows_all):
    rows, feats = feat.shape
    down = (((0,), (0,)), ((), ()))
    high, middle, low = pieces(freqs_ref[...])
    freqs = jnp.concatenate([high, middle, high, middle, low, high], axis=0)
    acc = None
    for at in range(0, rows, STEP_ROWS):
        high, middle, low = pieces(x_ref[:, at : at + STEP_ROWS])
        x = jnp.concatenate([high, high, middle, middle, high, low], axis=0)
        proj = lax.dot_general(x, freqs, down, preferred_element_type=jnp.float32) + phases_ref[...]
        scales = []
        for sub in range(STEP_ROWS // LANES):
            row = jnp.sqrt(weight_ref[pl.ds(at // LANES + sub, 1), :])
            scales.append(jnp.broadcast_to(row, (LANES, LANES)).T)
        scale = jnp.concatenate(scales, axis=0)
        scale = jnp.concatenate([scale] * (feats // LANES), axis=1)
        block = cosine(proj) * scale
        feat[at : at + STEP_ROWS, :] = block
        high, middle, low = pieces(block)
        part = lax.dot_general(high, jnp.concatenate([high, middle, low], axis=1), down, preferred_element_type=jnp.float32)
        cross = part[:, feats : 2 * feats] + part[:, 2 * feats :]
        even = part[:, :feats] + lax.dot_general(middle, middle, down, preferred_element_type=jnp.float32)
        acc = (even, cross) if acc is None else (acc[0] + even, acc[1] + cross)
    run = stored_ref[0] * jnp.where(root_ref[0] == me, 1.0, 0.0).astype(jnp.float32)
    running = lax.dot_general(run, run, down, precision=HIGHEST, preferred_element_type=jnp.float32)
    return running + (acc[0] + (acc[1] + acc[1].T)) * (1.0 / rows_all)


def triangles():
    row = lax.broadcasted_iota(jnp.int32, (LANES, LANES), 0)
    col = lax.broadcasted_iota(jnp.int32, (LANES, LANES), 1)
    return row, col


def pack(gram, mine):
    row, col = triangles()
    last = gram[LANES:, LANES:]
    squares = [jnp.where(row <= col, gram[:LANES, :LANES], last), gram[:LANES, LANES:]]
    diagonal = jnp.sum(jnp.where(row == col, last, 0.0), axis=0, keepdims=True)
    for side, square in enumerate(squares):
        for n in range(LANES // 4):
            mine[side, n, 0:4, :] = square[4 * n : 4 * n + 4]
            if side or n:
                mine[side, n, 4:5, :] = jnp.zeros((1, LANES), jnp.float32)
    mine[0, 0, 4:5, :] = diagonal


def unpack(chunks, a):
    row, col = triangles()
    squares = [jnp.concatenate([chunks[side, n, 0:4, :] for n in range(LANES // 4)], axis=0) for side in range(2)]
    mixed = squares[0]
    turned = mixed.T
    a[:LANES, :LANES] = jnp.where(row <= col, mixed, turned)
    a[:LANES, LANES:] = squares[1]
    a[LANES:, :LANES] = jnp.zeros((LANES, LANES), jnp.float32)
    a[LANES:, LANES:] = jnp.where(row > col, mixed, jnp.where(row < col, turned, chunks[0, 0, 4:5, :]))


def reduce_kernel(sizes, rows_all, *refs):
    sources, refs = refs[:6], refs[6:]
    loaded, load_sem, refs = refs[2:8], refs[8], refs[:2] + refs[9:]
    loads = [pltpu.make_async_copy(s, d, load_sem.at[n]) for n, (s, d) in enumerate(zip(sources, loaded))]
    for c in loads:
        c.start()
    reduce_loaded(sizes, rows_all, loads, *loaded, *refs)


def reduce_loaded(sizes, rows_all, loads, x_ref, freqs_ref, phases_ref, weight_ref, stored_ref, root_ref,
                  gram_out, feat_out, feat, mine, parts, zparts, done,
                  feat_sem, keep_sem, rs_send, rs_recv, z_send, z_recv, ag_send, ag_recv):
    nx, nz, ny = sizes
    grp, leaf = lax.axis_index("grp"), lax.axis_index("leaf")
    core, z, x = lax.rem(grp, 2), lax.rem(grp // 2, nz), grp // (2 * nz)

    def at(x_, z_, core_, y_):
        return ((x_ * nz + z_) * 2 + core_, y_)

    plane = []
    for dx in range(nx):
        for dy in range(ny):
            for dc in range(2):
                if dx or dy or dc:
                    plane.append((min(dx, nx - dx) + min(dy, ny - dy), dx, dy, dc))
    plane.sort(key=lambda t: -t[0])
    plane = [(lax.rem(x + dx, nx), lax.rem(leaf + dy, ny), lax.rem(core + dc, 2)) for _, dx, dy, dc in plane]
    line = sorted(range(1, nz), key=lambda d: -min(d, nz - d))
    line = [lax.rem(z + dz, nz) for dz in line]

    barrier = pltpu.get_barrier_semaphore()
    for px, py, pc in plane:
        pl.semaphore_signal(barrier, inc=1, device_id=at(px, z, pc, py), device_id_type=MESH)
    for pz in line:
        pl.semaphore_signal(barrier, inc=1, device_id=at(x, pz, core, leaf), device_id_type=MESH)

    me = grp * ny + leaf
    for c in loads:
        c.wait()
    gram = local_gram(x_ref, freqs_ref, phases_ref, weight_ref, stored_ref, root_ref, feat, me, rows_all)
    feat_copy = pltpu.make_async_copy(feat, feat_out, feat_sem)
    feat_copy.start()
    pack(gram, mine)

    pl.semaphore_wait(barrier, len(plane) + len(line))

    spot = x * ny + leaf
    copies = []
    for n, (px, py, pc) in enumerate(plane):
        copies.append(pltpu.make_async_remote_copy(
            mine.at[pc, px * ny + py], parts.at[n], rs_send.at[n], rs_recv.at[n],
            device_id=at(px, z, pc, py), device_id_type=MESH))
    for c in copies:
        c.start()
    total = mine[core, spot]
    for n in reversed(range(len(copies))):
        copies[n].wait_recv()
        total = total + parts[n]

    zparts[z] = total
    lines = []
    for n, pz in enumerate(line):
        lines.append(pltpu.make_async_remote_copy(
            zparts.at[z], zparts.at[z], z_send.at[n], z_recv.at[n],
            device_id=at(x, pz, core, leaf), device_id_type=MESH))
    for c in lines:
        c.start()
    for c in lines:
        c.wait_recv()
    total = zparts[0]
    for k in range(1, nz):
        total = total + zparts[k]

    done[...] = total
    spread = []
    for n, (px, py, pc) in enumerate(plane):
        spread.append(pltpu.make_async_remote_copy(
            done, gram_out.at[core, spot], ag_send.at[n], ag_recv.at[n],
            device_id=at(px, z, pc, py), device_id_type=MESH))
    for c in spread:
        c.start()
    keep = pltpu.make_async_copy(done, gram_out.at[core, spot], keep_sem)
    keep.start()
    for c in copies + lines + spread:
        c.wait_send()
    feat_copy.wait()
    keep.wait()
    for c in spread:
        c.wait_recv()


def columns(values, first, block):
    out = []
    for j in range(block):
        wide = jnp.broadcast_to(values[:, first + j : first + j + 1], (block, LANES))
        out.append([wide[8 * g : 8 * g + 8] for g in range(block // 8)])
    return out


def eliminate(a, factor, inverse, block):
    n = a.shape[0]
    groups = block // 8
    ntile = n // LANES
    sub8 = lax.broadcasted_iota(jnp.int32, (8, LANES), 0)
    rows_of = lax.broadcasted_iota(jnp.int32, (block, n), 0)
    cols_of = lax.broadcasted_iota(jnp.int32, (block, n), 1)

    def spread(part, g, s):
        return jnp.broadcast_to(part[g][s : s + 1], (8, LANES))

    def split(values):
        return [[values[8 * g : 8 * g + 8, LANES * t : LANES * t + LANES] for g in range(groups)] for t in range(values.shape[1] // LANES)]

    def within(cols, lo):
        return (cols >= lo) & (cols < lo + block)

    panel = a[0:block, :]
    drop = None
    for r0 in range(0, n, block):
        r1, r2 = r0 + block, r0 + 2 * block
        ahead = r1 < n
        col = columns(panel, r0, block)
        if ahead:
            base = (r1 // LANES) * LANES
            turned = panel[:, base : base + LANES].T[r1 - base : r2 - base, :]
            below = columns(turned, 0, block)
        lane0 = r0 % LANES
        eye = (cols_of[:, :LANES] == rows_of[:, :LANES] + lane0).astype(jnp.float32)
        row = split(panel) + split(eye)
        gone = [[None] * groups for _ in row]
        pivots = [None] * groups
        for k in range(block):
            gk, sk = divmod(k, 8)
            pivot = spread(col[0], 0, 0) if k == 0 else coming
            pivots[gk] = pivot if sk == 0 else jnp.where(sub8 >= sk, pivot, pivots[gk])
            inv = 1.0 / pivot
            if k + 1 < block:
                gn, sn = divmod(k + 1, 8)
                coming = spread(col[k + 1], gn, sn) - (spread(col[k], gn, sn) * spread(col[k + 1], gk, sk)) * inv
            mult = {}
            for g in range(gk, groups):
                if g == gk and sk == 7:
                    continue
                m = col[k][g] * inv
                if g == gk:
                    m = jnp.where(sub8 > sk, m, 0.0)
                mult[g] = m
            under = [below[k][g] * inv for g in range(groups)] if ahead else []
            for j in range(k + 1, block):
                lead = spread(col[j], gk, sk)
                for g, m in mult.items():
                    col[j][g] = col[j][g] - m * lead
                for g, m in enumerate(under):
                    below[j][g] = below[j][g] - m * lead
            for part, taken in zip(row, gone):
                lead = spread(part, gk, sk)
                for g, m in mult.items():
                    part[g] = part[g] - m * lead
                for g, m in enumerate(under):
                    taken[g] = m * lead if k == 0 else taken[g] + m * lead
        scale = [lax.rsqrt(p) for p in pivots]
        scaled = [jnp.concatenate([part[g] * scale[g] for g in range(groups)], axis=0) for part in row]
        full = jnp.concatenate(scaled[:ntile], axis=1)
        unit = jnp.concatenate([scaled[ntile]] * ntile, axis=1)
        upper = jnp.where(cols_of >= rows_of + r0, full, 0.0)
        factor[r0:r1, :] = upper
        lower = jnp.where(cols_of < r0, full, jnp.where(cols_of <= rows_of + r0, unit, 0.0))
        inverse[r0:r1, :] = lower
        if drop is not None and ahead:
            cols_rest = lax.broadcasted_iota(jnp.int32, (n - r1, n), 1)
            a[r1:, :] = jnp.where(within(cols_rest, r0 - block), 0.0, a[r1:, :]) - drop
        if r2 < n:
            both = jnp.where(cols_of >= r1, full, lower)
            high, middle, low = pieces(upper)
            left = jnp.concatenate([high, high, middle, middle, high, low], axis=0).T[r2:, :]
            high, middle, low = pieces(both)
            right = jnp.concatenate([high, middle, high, middle, low, high], axis=0)
            drop = jnp.dot(left, right, preferred_element_type=jnp.float32)
        if ahead:
            taken = [jnp.concatenate(part, axis=0) for part in gone]
            rest = jnp.concatenate(taken[:ntile], axis=1)
            own = jnp.concatenate([taken[ntile]] * ntile, axis=1)
            here = within(cols_of, r0)
            panel = jnp.where(here, 0.0, a[r1:r2, :]) - jnp.where(here, own, rest)


def basis_kernel(gram_in, feat_in, factor_out, basis_out, gram, a, factor, inverse, feat, out, in_sem, factor_sem, out_sem):
    first = pltpu.make_async_copy(gram_in, gram, in_sem.at[0])
    first.start()
    load = pltpu.make_async_copy(feat_in, feat, in_sem.at[1])
    load.start()
    first.wait()
    unpack(gram, a)
    eliminate(a, factor, inverse, BLOCK)
    copies = [pltpu.make_async_copy(factor, factor_out, factor_sem)]
    copies[0].start()
    right = inverse[...].T
    load.wait()
    rows = feat.shape[0]
    for n, at in enumerate(range(0, rows, TILE_ROWS)):
        tile = pl.ds(at, TILE_ROWS)
        out[tile, :] = jnp.dot(feat[tile, :], right, precision=HIGHEST, preferred_element_type=jnp.float32)
        c = pltpu.make_async_copy(out.at[tile, :], basis_out.at[tile, :], out_sem.at[n])
        c.start()
        copies.append(c)
    for c in copies:
        c.wait()


VMEM = functools.partial(pl.BlockSpec, memory_space=pltpu.VMEM)
HBM = functools.partial(pl.BlockSpec, memory_space=pltpu.HBM)


def run_basis(gram, features):
    rows, feats = features.shape
    f32 = jnp.float32
    square = pltpu.VMEM((feats, feats), f32)
    return pl.pallas_call(
        basis_kernel,
        out_shape=(jax.ShapeDtypeStruct((feats, feats), f32), jax.ShapeDtypeStruct((rows, feats), f32)),
        in_specs=[HBM(), HBM()],
        out_specs=(HBM(), HBM()),
        scratch_shapes=[
            pltpu.VMEM(gram.shape, f32),
            square, square, square,
            pltpu.VMEM((rows, feats), f32),
            pltpu.VMEM((rows, feats), f32),
            pltpu.SemaphoreType.DMA((2,)),
            pltpu.SemaphoreType.DMA,
            pltpu.SemaphoreType.DMA((rows // TILE_ROWS,)),
        ],
        compiler_params=pltpu.CompilerParams(vmem_limit_bytes=60 * 2**20),
        name="basis",
    )(gram, features)


def per_device(sizes, rows_all, inputs, freqs, phases, sample_weight, stored, root):
    rows, feats = inputs.shape[0], freqs.shape[1]
    nx, nz, ny = sizes
    f32 = jnp.float32
    nplane, nline = 2 * nx * ny - 1, nz - 1
    chunks = LANES // 4
    dma = pltpu.SemaphoreType.DMA
    gram, features = pl.pallas_call(
        functools.partial(reduce_kernel, sizes, rows_all),
        out_shape=(jax.ShapeDtypeStruct((2, chunks, CHUNK_ROWS, LANES), f32), jax.ShapeDtypeStruct((rows, feats), f32)),
        in_specs=[HBM()] * 6,
        out_specs=(HBM(), HBM()),
        scratch_shapes=[
            pltpu.VMEM((inputs.shape[1], rows), f32),
            pltpu.VMEM(freqs.shape, f32),
            pltpu.VMEM((1, feats), f32),
            pltpu.VMEM((rows // LANES, LANES), f32),
            pltpu.VMEM(stored.shape, f32),
            pltpu.SMEM(root.shape, jnp.int32),
            dma((6,)),
            pltpu.VMEM((rows, feats), f32),
            pltpu.VMEM((2, chunks, CHUNK_ROWS, LANES), f32),
            pltpu.VMEM((nplane, CHUNK_ROWS, LANES), f32),
            pltpu.VMEM((nz, CHUNK_ROWS, LANES), f32),
            pltpu.VMEM((CHUNK_ROWS, LANES), f32),
            dma, dma,
            dma((nplane,)), dma((nplane,)),
            dma((nline,)), dma((nline,)),
            dma((nplane,)), dma((nplane,)),
        ],
        compiler_params=pltpu.CompilerParams(collective_id=0, has_side_effects=True, vmem_limit_bytes=60 * 2**20),
        name="reduce",
    )(inputs.T, freqs, phases[None, :], sample_weight.reshape(rows // LANES, LANES), stored, root)
    return run_basis(gram, features)


def solution(mesh):
    groups, leaves = mesh.shape["grp"], mesh.shape["leaf"]
    nx = LANES // 4 // leaves
    sizes = (nx, groups // 2 // nx, leaves)
    return jax.shard_map(
        lambda inputs, *rest: per_device(sizes, inputs.shape[0] * groups * leaves, inputs, *rest),
        mesh=mesh,
        in_specs=(
            P(("grp", "leaf"), None),
            P(),
            P(),
            P(("grp", "leaf")),
            P(("grp", "leaf"), None, None),
            P(),
        ),
        out_specs=(P(), P(("grp", "leaf"), None)),
        check_vma=False,
    )
```

```python
import functools
import math

import jax
import jax.numpy as jnp
import numpy as np
from jax import lax
from jax.experimental import pallas as pl
from jax.experimental.pallas import tpu as pltpu
from jax.sharding import PartitionSpec as P

MESH = pl.DeviceIdType.MESH
HIGHEST = lax.Precision.HIGHEST
LANES = 128
BLOCK = 16
TILE_ROWS = 256
STEP_ROWS = 1024
CHUNK_ROWS = 5

TWO_PI_HI = float(np.float32(round(2 * math.pi * 2**15) / 2**15))
TWO_PI_LO = float(np.float32(2 * math.pi - TWO_PI_HI))


def half_sine_coefs():
    top = (math.pi * 1.001) ** 2
    nodes = top * (0.5 + 0.5 * np.cos((np.arange(64) + 0.5) * math.pi / 64))
    roots = np.sqrt(nodes)
    values = math.sqrt(2.0) * np.sin(roots / 2) / roots
    fit = np.polynomial.chebyshev.Chebyshev.fit(nodes, values, 4, domain=[0, top])
    power = fit.convert(kind=np.polynomial.Polynomial)
    return [float(c) for c in power.coef]


COEFS = half_sine_coefs()


def cosine(x):
    turns = jnp.round(x * (1.0 / (2 * math.pi)))
    r = (x - turns * TWO_PI_HI) - turns * TWO_PI_LO
    t = r * r
    poly = jnp.full_like(t, COEFS[-1])
    for c in COEFS[-2::-1]:
        poly = poly * t + c
    s = r * poly
    return 1.0 - s * s


def pieces(x):
    high = x.astype(jnp.bfloat16)
    rest = x - high.astype(jnp.float32)
    middle = rest.astype(jnp.bfloat16)
    return high, middle, (rest - middle.astype(jnp.float32)).astype(jnp.bfloat16)


def local_gram(x_ref, freqs_ref, phases_ref, weight_ref, stored_ref, root_ref, feat, me, rows_all):
    rows, feats = feat.shape
    down = (((0,), (0,)), ((), ()))
    high, middle, low = pieces(freqs_ref[...])
    freqs = jnp.concatenate([high, middle, high, middle, low, high], axis=0)
    acc = None
    for at in range(0, rows, STEP_ROWS):
        high, middle, low = pieces(x_ref[:, at : at + STEP_ROWS])
        x = jnp.concatenate([high, high, middle, middle, high, low], axis=0)
        proj = lax.dot_general(x, freqs, down, preferred_element_type=jnp.float32) + phases_ref[...]
        scales = []
        for sub in range(STEP_ROWS // LANES):
            row = jnp.sqrt(weight_ref[pl.ds(at // LANES + sub, 1), :])
            scales.append(jnp.broadcast_to(row, (LANES, LANES)).T)
        scale = jnp.concatenate(scales, axis=0)
        scale = jnp.concatenate([scale] * (feats // LANES), axis=1)
        block = cosine(proj) * scale
        feat[at : at + STEP_ROWS, :] = block
        high, middle, low = pieces(block)
        part = lax.dot_general(high, jnp.concatenate([high, middle, low], axis=1), down, preferred_element_type=jnp.float32)
        cross = part[:, feats : 2 * feats] + part[:, 2 * feats :]
        even = part[:, :feats] + lax.dot_general(middle, middle, down, preferred_element_type=jnp.float32)
        acc = (even, cross) if acc is None else (acc[0] + even, acc[1] + cross)
    run = stored_ref[0] * jnp.where(root_ref[0] == me, 1.0, 0.0).astype(jnp.float32)
    running = lax.dot_general(run, run, down, precision=HIGHEST, preferred_element_type=jnp.float32)
    return running + (acc[0] + (acc[1] + acc[1].T)) * (1.0 / rows_all)


def triangles():
    row = lax.broadcasted_iota(jnp.int32, (LANES, LANES), 0)
    col = lax.broadcasted_iota(jnp.int32, (LANES, LANES), 1)
    return row, col


def pack(gram, mine):
    row, col = triangles()
    last = gram[LANES:, LANES:]
    squares = [jnp.where(row <= col, gram[:LANES, :LANES], last), gram[:LANES, LANES:]]
    diagonal = jnp.sum(jnp.where(row == col, last, 0.0), axis=0, keepdims=True)
    for side, square in enumerate(squares):
        for n in range(LANES // 4):
            mine[side, n, 0:4, :] = square[4 * n : 4 * n + 4]
            if side or n:
                mine[side, n, 4:5, :] = jnp.zeros((1, LANES), jnp.float32)
    mine[0, 0, 4:5, :] = diagonal


def unpack(chunks, a):
    row, col = triangles()
    squares = [jnp.concatenate([chunks[side, n, 0:4, :] for n in range(LANES // 4)], axis=0) for side in range(2)]
    mixed = squares[0]
    turned = mixed.T
    a[:LANES, :LANES] = jnp.where(row <= col, mixed, turned)
    a[:LANES, LANES:] = squares[1]
    a[LANES:, :LANES] = jnp.zeros((LANES, LANES), jnp.float32)
    a[LANES:, LANES:] = jnp.where(row > col, mixed, jnp.where(row < col, turned, chunks[0, 0, 4:5, :]))


def reduce_kernel(sizes, rows_all, *refs):
    sources, refs = refs[:6], refs[6:]
    loaded, load_sem, refs = refs[2:8], refs[8], refs[:2] + refs[9:]
    loads = [pltpu.make_async_copy(s, d, load_sem.at[n]) for n, (s, d) in enumerate(zip(sources, loaded))]
    for c in loads:
        c.start()
    reduce_loaded(sizes, rows_all, loads, *loaded, *refs)


def reduce_loaded(sizes, rows_all, loads, x_ref, freqs_ref, phases_ref, weight_ref, stored_ref, root_ref,
                  gram_out, feat_out, feat, mine, theirs, half, parts, zparts, back,
                  feat_sem, core_send, core_recv, rs_send, rs_recv, z_send, z_recv, ag_send, ag_recv, end_send, end_recv, keep_sem):
    nx, nz, ny = sizes
    grp, leaf = lax.axis_index("grp"), lax.axis_index("leaf")
    core, z, x = lax.rem(grp, 2), lax.rem(grp // 2, nz), grp // (2 * nz)

    def at(x_, z_, core_, y_):
        return ((x_ * nz + z_) * 2 + core_, y_)

    other = at(x, z, 1 - core, leaf)
    plane = []
    for dx in range(nx):
        for dy in range(ny):
            if dx or dy:
                plane.append((min(dx, nx - dx) + min(dy, ny - dy), dx, dy))
    plane.sort(key=lambda t: -t[0])
    plane = [(lax.rem(x + dx, nx), lax.rem(leaf + dy, ny)) for _, dx, dy in plane]
    line = sorted(range(1, nz), key=lambda d: -min(d, nz - d))
    line = [lax.rem(z + dz, nz) for dz in line]

    barrier = pltpu.get_barrier_semaphore()
    pl.semaphore_signal(barrier, inc=1, device_id=other, device_id_type=MESH)
    for px, py in plane:
        pl.semaphore_signal(barrier, inc=1, device_id=at(px, z, core, py), device_id_type=MESH)
    for pz in line:
        pl.semaphore_signal(barrier, inc=1, device_id=at(x, pz, core, leaf), device_id_type=MESH)

    me = grp * ny + leaf
    for c in loads:
        c.wait()
    gram = local_gram(x_ref, freqs_ref, phases_ref, weight_ref, stored_ref, root_ref, feat, me, rows_all)
    feat_copy = pltpu.make_async_copy(feat, feat_out, feat_sem)
    feat_copy.start()
    pack(gram, mine)

    pl.semaphore_wait(barrier, 1 + len(plane) + len(line))

    swap = pltpu.make_async_remote_copy(mine.at[1 - core], theirs, core_send, core_recv, device_id=other, device_id_type=MESH)
    swap.start()
    swap.wait_recv()
    half[...] = mine[core] + theirs[...]

    spot = x * ny + leaf
    copies = []
    for n, (px, py) in enumerate(plane):
        there = px * ny + py
        copies.append(pltpu.make_async_remote_copy(
            half.at[there], parts.at[n], rs_send.at[n], rs_recv.at[n],
            device_id=at(px, z, core, py), device_id_type=MESH))
    for c in copies:
        c.start()
    total = half[spot]
    for n in reversed(range(len(copies))):
        copies[n].wait_recv()
        total = total + parts[n]

    zparts[z] = total
    lines = []
    for n, pz in enumerate(line):
        lines.append(pltpu.make_async_remote_copy(
            zparts.at[z], zparts.at[z], z_send.at[n], z_recv.at[n],
            device_id=at(x, pz, core, leaf), device_id_type=MESH))
    for c in lines:
        c.start()
    for c in lines:
        c.wait_recv()
    total = zparts[0]
    for k in range(1, nz):
        total = total + zparts[k]

    back[spot] = total
    spread = []
    for n, (px, py) in enumerate(plane):
        spread.append(pltpu.make_async_remote_copy(
            back.at[spot], back.at[spot], ag_send.at[n], ag_recv.at[n],
            device_id=at(px, z, core, py), device_id_type=MESH))
    for c in spread:
        c.start()
    for c in spread:
        c.wait_recv()

    end = pltpu.make_async_remote_copy(back, gram_out.at[core], end_send, end_recv, device_id=other, device_id_type=MESH)
    end.start()
    keep = pltpu.make_async_copy(back, gram_out.at[core], keep_sem)
    keep.start()
    for c in [swap] + copies + lines + spread:
        c.wait_send()
    feat_copy.wait()
    keep.wait()
    end.wait()


def columns(values, first, block):
    out = []
    for j in range(block):
        wide = jnp.broadcast_to(values[:, first + j : first + j + 1], (block, LANES))
        out.append([wide[8 * g : 8 * g + 8] for g in range(block // 8)])
    return out


def eliminate(a, factor, inverse, block):
    n = a.shape[0]
    groups = block // 8
    ntile = n // LANES
    sub8 = lax.broadcasted_iota(jnp.int32, (8, LANES), 0)
    rows_of = lax.broadcasted_iota(jnp.int32, (block, n), 0)
    cols_of = lax.broadcasted_iota(jnp.int32, (block, n), 1)

    def spread(part, g, s):
        return jnp.broadcast_to(part[g][s : s + 1], (8, LANES))

    def split(values):
        return [[values[8 * g : 8 * g + 8, LANES * t : LANES * t + LANES] for g in range(groups)] for t in range(values.shape[1] // LANES)]

    def within(cols, lo):
        return (cols >= lo) & (cols < lo + block)

    panel = a[0:block, :]
    drop = None
    for r0 in range(0, n, block):
        r1, r2 = r0 + block, r0 + 2 * block
        ahead = r1 < n
        col = columns(panel, r0, block)
        if ahead:
            base = (r1 // LANES) * LANES
            turned = panel[:, base : base + LANES].T[r1 - base : r2 - base, :]
            below = columns(turned, 0, block)
        lane0 = r0 % LANES
        eye = (cols_of[:, :LANES] == rows_of[:, :LANES] + lane0).astype(jnp.float32)
        row = split(panel) + split(eye)
        gone = [[None] * groups for _ in row]
        pivots = [None] * groups
        for k in range(block):
            gk, sk = divmod(k, 8)
            pivot = spread(col[0], 0, 0) if k == 0 else coming
            pivots[gk] = pivot if sk == 0 else jnp.where(sub8 >= sk, pivot, pivots[gk])
            inv = 1.0 / pivot
            if k + 1 < block:
                gn, sn = divmod(k + 1, 8)
                coming = spread(col[k + 1], gn, sn) - (spread(col[k], gn, sn) * spread(col[k + 1], gk, sk)) * inv
            mult = {}
            for g in range(gk, groups):
                if g == gk and sk == 7:
                    continue
                m = col[k][g] * inv
                if g == gk:
                    m = jnp.where(sub8 > sk, m, 0.0)
                mult[g] = m
            under = [below[k][g] * inv for g in range(groups)] if ahead else []
            for j in range(k + 1, block):
                lead = spread(col[j], gk, sk)
                for g, m in mult.items():
                    col[j][g] = col[j][g] - m * lead
                for g, m in enumerate(under):
                    below[j][g] = below[j][g] - m * lead
            for part, taken in zip(row, gone):
                lead = spread(part, gk, sk)
                for g, m in mult.items():
                    part[g] = part[g] - m * lead
                for g, m in enumerate(under):
                    taken[g] = m * lead if k == 0 else taken[g] + m * lead
        scale = [lax.rsqrt(p) for p in pivots]
        scaled = [jnp.concatenate([part[g] * scale[g] for g in range(groups)], axis=0) for part in row]
        full = jnp.concatenate(scaled[:ntile], axis=1)
        unit = jnp.concatenate([scaled[ntile]] * ntile, axis=1)
        upper = jnp.where(cols_of >= rows_of + r0, full, 0.0)
        factor[r0:r1, :] = upper
        lower = jnp.where(cols_of < r0, full, jnp.where(cols_of <= rows_of + r0, unit, 0.0))
        inverse[r0:r1, :] = lower
        if drop is not None and ahead:
            cols_rest = lax.broadcasted_iota(jnp.int32, (n - r1, n), 1)
            a[r1:, :] = jnp.where(within(cols_rest, r0 - block), 0.0, a[r1:, :]) - drop
        if r2 < n:
            both = jnp.where(cols_of >= r1, full, lower)
            high, middle, low = pieces(upper)
            left = jnp.concatenate([high, high, middle, middle, high, low], axis=0).T[r2:, :]
            high, middle, low = pieces(both)
            right = jnp.concatenate([high, middle, high, middle, low, high], axis=0)
            drop = jnp.dot(left, right, preferred_element_type=jnp.float32)
        if ahead:
            taken = [jnp.concatenate(part, axis=0) for part in gone]
            rest = jnp.concatenate(taken[:ntile], axis=1)
            own = jnp.concatenate([taken[ntile]] * ntile, axis=1)
            here = within(cols_of, r0)
            panel = jnp.where(here, 0.0, a[r1:r2, :]) - jnp.where(here, own, rest)


def basis_kernel(gram_in, feat_in, factor_out, basis_out, gram, a, factor, inverse, feat, out, in_sem, factor_sem, out_sem):
    first = pltpu.make_async_copy(gram_in, gram, in_sem.at[0])
    first.start()
    load = pltpu.make_async_copy(feat_in, feat, in_sem.at[1])
    load.start()
    first.wait()
    unpack(gram, a)
    eliminate(a, factor, inverse, BLOCK)
    copies = [pltpu.make_async_copy(factor, factor_out, factor_sem)]
    copies[0].start()
    right = inverse[...].T
    load.wait()
    rows = feat.shape[0]
    for n, at in enumerate(range(0, rows, TILE_ROWS)):
        tile = pl.ds(at, TILE_ROWS)
        out[tile, :] = jnp.dot(feat[tile, :], right, precision=HIGHEST, preferred_element_type=jnp.float32)
        c = pltpu.make_async_copy(out.at[tile, :], basis_out.at[tile, :], out_sem.at[n])
        c.start()
        copies.append(c)
    for c in copies:
        c.wait()


VMEM = functools.partial(pl.BlockSpec, memory_space=pltpu.VMEM)
HBM = functools.partial(pl.BlockSpec, memory_space=pltpu.HBM)


def run_basis(gram, features):
    rows, feats = features.shape
    f32 = jnp.float32
    square = pltpu.VMEM((feats, feats), f32)
    return pl.pallas_call(
        basis_kernel,
        out_shape=(jax.ShapeDtypeStruct((feats, feats), f32), jax.ShapeDtypeStruct((rows, feats), f32)),
        in_specs=[HBM(), HBM()],
        out_specs=(HBM(), HBM()),
        scratch_shapes=[
            pltpu.VMEM(gram.shape, f32),
            square, square, square,
            pltpu.VMEM((rows, feats), f32),
            pltpu.VMEM((rows, feats), f32),
            pltpu.SemaphoreType.DMA((2,)),
            pltpu.SemaphoreType.DMA,
            pltpu.SemaphoreType.DMA((rows // TILE_ROWS,)),
        ],
        compiler_params=pltpu.CompilerParams(vmem_limit_bytes=60 * 2**20),
        name="basis",
    )(gram, features)


def per_device(sizes, rows_all, inputs, freqs, phases, sample_weight, stored, root):
    rows, feats = inputs.shape[0], freqs.shape[1]
    nx, nz, ny = sizes
    f32 = jnp.float32
    nplane, nline = nx * ny - 1, nz - 1
    chunks = LANES // 4
    dma = pltpu.SemaphoreType.DMA
    gram, features = pl.pallas_call(
        functools.partial(reduce_kernel, sizes, rows_all),
        out_shape=(jax.ShapeDtypeStruct((2, chunks, CHUNK_ROWS, LANES), f32), jax.ShapeDtypeStruct((rows, feats), f32)),
        in_specs=[HBM()] * 6,
        out_specs=(HBM(), HBM()),
        scratch_shapes=[
            pltpu.VMEM((inputs.shape[1], rows), f32),
            pltpu.VMEM(freqs.shape, f32),
            pltpu.VMEM((1, feats), f32),
            pltpu.VMEM((rows // LANES, LANES), f32),
            pltpu.VMEM(stored.shape, f32),
            pltpu.SMEM(root.shape, jnp.int32),
            dma((6,)),
            pltpu.VMEM((rows, feats), f32),
            pltpu.VMEM((2, chunks, CHUNK_ROWS, LANES), f32),
            pltpu.VMEM((chunks, CHUNK_ROWS, LANES), f32),
            pltpu.VMEM((chunks, CHUNK_ROWS, LANES), f32),
            pltpu.VMEM((nplane, CHUNK_ROWS, LANES), f32),
            pltpu.VMEM((nz, CHUNK_ROWS, LANES), f32),
            pltpu.VMEM((chunks, CHUNK_ROWS, LANES), f32),
            dma, dma, dma,
            dma((nplane,)), dma((nplane,)),
            dma((nline,)), dma((nline,)),
            dma((nplane,)), dma((nplane,)),
            dma, dma, dma,
        ],
        compiler_params=pltpu.CompilerParams(collective_id=0, has_side_effects=True, vmem_limit_bytes=60 * 2**20),
        name="reduce",
    )(inputs.T, freqs, phases[None, :], sample_weight.reshape(rows // LANES, LANES), stored, root)
    return run_basis(gram, features)


def solution(mesh):
    groups, leaves = mesh.shape["grp"], mesh.shape["leaf"]
    nx = LANES // 4 // leaves
    sizes = (nx, groups // 2 // nx, leaves)
    return jax.shard_map(
        lambda inputs, *rest: per_device(sizes, inputs.shape[0] * groups * leaves, inputs, *rest),
        mesh=mesh,
        in_specs=(
            P(("grp", "leaf"), None),
            P(),
            P(),
            P(("grp", "leaf")),
            P(("grp", "leaf"), None, None),
            P(),
        ),
        out_specs=(P(), P(("grp", "leaf"), None)),
        check_vma=False,
    )
```
